32 devices in a mesh: scen: 4 (over x, core), col: 8 (over z, y).
Axes of the slice: x: 2, y: 2, z: 4, core: 2. Of those that a mesh axis runs over, the one named last changes fastest.
Arguments:
- coupling: float32 [4, 512, 16384], P('scen', None, 'col'), may hold values from -0.25 to 0.25
- inverse_slabs: float32 [4, 512, 512], P('scen', 'col'), as said below
- barrier_diagonal: float32 [16384], replicated, may hold values from 1 to 16
Outputs:
- panel_factor: float32 [16384, 256], P('col')
The draws below stay inside these ranges and needn't reach their ends.
Inputs may be any that keep to these rules, and one draw needn't show every extreme that they name: `inverse_slabs`: each slab is symmetric positive definite.
All inputs are finite; a program needn't handle non-finite values.
Results may differ from the reference program's by a relative error of at most 0.0001.
Values sent between devices are 32-bit elements; how exact they have to be, the bound alone decides.
A program may use at most 64 MiB of HBM per device.

```python
import math
import jax
import jax.numpy as jnp
from jax import lax

K = 512
NV = 16384
PANEL = 256
SCEN = 4


def draw_inverse_slabs(key, part):
    base_key = jax.random.fold_in(key, 7)
    key_diag, key_mix = jax.random.split(base_key)
    diag_values = jnp.exp(jax.random.uniform(key_diag, (SCEN, K), jnp.float32, math.log(0.5), math.log(8.0)))
    mixing = jax.random.normal(key_mix, (SCEN, K, K), jnp.float32)

    def one_slab(slab_pair):
        mix_matrix, values = slab_pair
        gram = jnp.dot(mix_matrix, mix_matrix.T, precision=lax.Precision.HIGHEST) / K
        return 0.5 * (gram + gram.T) + jnp.diag(values)
    return lax.map(one_slab, (mixing, diag_values))


def block_levels(key, extent, cuts, least, largest):
    def one(position, blocks):
        heights = jax.random.uniform(jax.random.fold_in(jax.random.fold_in(key, 6), position), (blocks,), jnp.float32, least / len(cuts), largest / len(cuts))
        return jnp.repeat(jnp.exp(heights), extent[position] // blocks).reshape((-1,) + (1,) * (len(extent) - position - 1))

    loudness = one(*cuts[0])
    for cut in cuts[1:]:
        loudness = loudness * one(*cut)
    return loudness


def gaussian(own_key, shape, spread, reach, cuts=(), kind=jnp.bfloat16):
    loudness = block_levels(own_key, shape, cuts, -0.22, 0.18) if cuts else 1.0
    drawn = jax.random.normal(own_key, shape, jnp.float32) * spread * loudness
    return jnp.minimum(jnp.maximum(drawn, -reach), reach).astype(kind)


def setup_inputs(seed: int = 0) -> dict:
    seeds = jax.random.split(jax.random.key(seed), 4)
    return {
        "coupling": gaussian(seeds[0], (SCEN, K, NV), K ** -0.5, 0.25, ((0, 4), (2, 8)), jnp.float32),
        "inverse_slabs": draw_inverse_slabs(jax.random.fold_in(seeds[3], 71), 0),
        "barrier_diagonal": jnp.clip(jnp.exp(jax.random.uniform(seeds[2], (NV,), jnp.float32, math.log(1.0), math.log(16.0))), 1.0, 16.0),
    }


def reference(coupling, inverse_slabs, barrier_diagonal):

    def one_scenario(running, scenario_pair):
        block_matrix, inverse_block = scenario_pair
        solved = jnp.dot(inverse_block.astype(jnp.float32), block_matrix[:, :PANEL].astype(jnp.float32), precision=lax.Precision.HIGHEST, preferred_element_type=jnp.float32)
        update = jnp.dot(block_matrix.T.astype(jnp.float32), solved.astype(jnp.float32), precision=lax.Precision.HIGHEST, preferred_element_type=jnp.float32)
        return (running + update, None)
    partial_value, _ = lax.scan(one_scenario, jnp.zeros((NV, PANEL), jnp.float32), (coupling, inverse_slabs))
    row_ids = jnp.arange(NV, dtype=jnp.int32)[:, None]
    col_ids = jnp.arange(PANEL, dtype=jnp.int32)[None, :]
    schur_rows = partial_value + jnp.where(row_ids == col_ids, barrier_diagonal[:, None], jnp.zeros_like(partial_value))
    top_rows = schur_rows[:PANEL]
    pivot_matrix = 0.5 * (top_rows + top_rows.T)
    factor = jnp.linalg.cholesky(pivot_matrix)
    solved_rows = jax.scipy.linalg.solve_triangular(factor, schur_rows.T, lower=True).T
    return jnp.concatenate([factor, solved_rows[PANEL:]], axis=0)
```

```python
import functools

import jax
import jax.numpy as jnp
from jax import lax
from jax.experimental import pallas as pl
from jax.experimental.pallas import tpu as pltpu
from jax.sharding import PartitionSpec as P

PANEL = 256
HALF = PANEL // 2
QUEUE = 8
MESH = pl.DeviceIdType.MESH
HI = lax.Precision.HIGHEST
F32 = jnp.float32
BF16 = jnp.bfloat16


def split(value):
    high = value.astype(BF16)
    return high, (value - high.astype(F32)).astype(BF16)


def dot(a, b):
    return jnp.dot(a, b, preferred_element_type=F32)


def full(a, b, dims=((1,), (0,))):
    return lax.dot_general(a, b, (dims, ((), ())), precision=HI, preferred_element_type=F32)


def factor_block(a, step=2):
    size = a.shape[0]
    row = lax.broadcasted_iota(jnp.int32, (size, size), 0)
    col = lax.broadcasted_iota(jnp.int32, (size, size), 1)
    left, right = a, jnp.where(row == col, 1.0, 0.0).astype(F32)
    for k in range(0, size, step):
        base = k // 8 * 8
        l_live, r_live = left[base:], right[base:]
        rows = lax.broadcasted_iota(jnp.int32, (size - base, 1), 0) + base
        cols = [
            jnp.broadcast_to(l_live[:, k + t : k + t + 1], (size - base, size)) for t in range(step)
        ]
        lrows = [l_live[k + t - base : k + t + 1 - base] for t in range(step)]
        rrows = [r_live[k + t - base : k + t + 1 - base] for t in range(step)]
        for t in range(step):
            at = k + t - base
            inv = 1.0 / cols[t][at : at + 1]
            fac = jnp.where(rows > k + t, cols[t] * inv, 0.0)
            for u in range(t + 1, step):
                au = k + u - base
                cols[u] = cols[u] - fac * cols[u][at : at + 1]
                lrows[u] = lrows[u] - fac[au : au + 1] * lrows[t]
                rrows[u] = rrows[u] - fac[au : au + 1] * rrows[t]
            l_live = l_live - fac * lrows[t]
            r_live = r_live - fac * rrows[t]
        if base:
            left = jnp.concatenate([left[:base], l_live], axis=0)
            right = jnp.concatenate([right[:base], r_live], axis=0)
        else:
            left, right = l_live, r_live
    diag = jnp.sum(jnp.where(row == col, left, 0.0), axis=1, keepdims=True)
    scale = 1.0 / jnp.sqrt(diag)
    return jnp.where(row <= col, left * scale, 0.0), right * scale


def kernel(
    n_scen, n_col, pieces, c_ref, h_ref, d_ref, out_ref,
    cbuf, hbuf, pbuf, chi, clo, sendbuf, acc, crecv, xrecv, xout,
    piv, pivc, pivb, pivx,
    lsem, hsend, hrecv, psend, precv, csend, crsem, xsend, xrsem, osend, orsem, vsend, vrecv,
):
    scen, col = lax.axis_index("scen"), lax.axis_index("col")
    depth, n = cbuf.shape
    share = h_ref.shape[1]
    half = n // 2
    rows = half // pieces
    core = lax.rem(scen, 2)
    col_bits = [1 << i for i in reversed(range((n_col - 1).bit_length()))]
    scen_bits = [1 << i for i in range((n_scen - 1).bit_length())]

    def flip(index, bit):
        return jnp.where(lax.rem(index // bit, 2) == 0, index + bit, index - bit)

    def xor(index, mask):
        for b in col_bits:
            if mask & b:
                index = flip(index, b)
        return index

    def remote(src, dst, send, recv, who):
        return pltpu.make_async_remote_copy(
            src_ref=src, dst_ref=dst, send_sem=send, recv_sem=recv, device_id=who, device_id_type=MESH
        )

    load_c = pltpu.make_async_copy(c_ref.at[0], cbuf, lsem.at[0])
    load_c.start()
    load_h = pltpu.make_async_copy(
        h_ref.at[0], hbuf.at[pl.ds(pl.multiple_of(col * share, share), share)], lsem.at[1]
    )
    load_h.start()

    barrier = pltpu.get_barrier_semaphore()
    peers = [(scen, flip(col, b)) for b in col_bits]
    peers += [(scen, lax.rem(col + 2, n_col)), (scen, lax.rem(col + n_col - 2, n_col))]
    peers += [(flip(scen, b), col) for b in scen_bits]
    for peer in peers:
        pl.semaphore_signal(barrier, inc=1, device_id=peer, device_id_type=MESH)
    pl.semaphore_wait(barrier, len(peers))

    h_copies = []

    def h_send(d):
        owner = xor(col, d)
        where = hbuf.at[pl.ds(pl.multiple_of(owner * share, share), share)]
        for b in col_bits:
            if d == 0 or b < (d & -d):
                copy = remote(where, where, hsend.at[len(h_copies)], hrecv.at[d | b], (scen, flip(col, b)))
                copy.start()
                h_copies.append(copy)

    def h_wait(d):
        owner = xor(col, d)
        where = hbuf.at[pl.ds(pl.multiple_of(owner * share, share), share)]
        remote(where, where, hsend.at[0], hrecv.at[d], (scen, flip(col, 1))).wait_recv()

    even = lax.rem(col, 2) == 0
    along = jnp.logical_and(even, col + 2 < n_col)
    prow = depth // QUEUE

    def p_copy(q, which):
        where = pbuf.at[pl.ds(q * prow, prow)]
        target = lax.rem(col + 2, n_col) if which == 0 else flip(col, 1)
        return remote(where, where, psend.at[q, which], precv.at[q], (scen, target))

    def p_send(q):
        @pl.when(along)
        def _():
            p_copy(q, 0).start()

        @pl.when(even)
        def _():
            p_copy(q, 1).start()

    load_h.wait()
    h_send(0)
    load_c.wait()

    @pl.when(col == 0)
    def _():
        pbuf[...] = cbuf[:, :PANEL]

    blocks = n // 128
    order = sorted(range(1, n_col), key=lambda d: (bin(d).count("1"), -d))
    total = max(len(order), QUEUE)
    done = 0
    for i in range(total):
        for q in range(i * QUEUE // total, (i + 1) * QUEUE // total):
            @pl.when(col != 0)
            def _(q=q):
                p_copy(q, 1).wait_recv()
            p_send(q)
        for at in range(i * len(order) // total, (i + 1) * len(order) // total):
            h_wait(order[at])
            h_send(order[at])
        for j in range(i * blocks // total, (i + 1) * blocks // total):
            high, low = split(cbuf[:, j * 128 : (j + 1) * 128].T)
            chi[j * 128 : (j + 1) * 128] = high
            clo[j * 128 : (j + 1) * 128] = low

    panel = pbuf[...]
    solved = full(hbuf[...], panel)
    s_hi, s_lo = split(solved)
    panel_t = panel.T
    top = full(panel_t[:HALF], solved)
    piv[0:HALF] = top[:, :HALF]
    piv[HALF : 2 * HALF] = top[:, HALF:]
    piv[2 * HALF : 3 * HALF] = full(panel_t[HALF:], solved[:, HALF:])
    vrows = 3 * HALF // 2
    mine = pl.multiple_of(core * vrows, vrows)
    theirs = pl.multiple_of((1 - core) * vrows, vrows)
    pair = (flip(scen, 1), col)
    v0 = remote(piv.at[pl.ds(theirs, vrows)], pivc, vsend.at[0], vrecv.at[0], pair)
    v0.start()

    def term(start):
        start = pl.multiple_of(start, rows)
        high, low = chi[pl.ds(start, rows)], clo[pl.ds(start, rows)]
        return dot(high, s_hi) + (dot(high, s_lo) + dot(low, s_hi))

    c_copies = []
    for p in range(pieces):
        sendbuf[p] = term((1 - core) * half + p * rows)
        copy = remote(sendbuf.at[p], crecv.at[p], csend.at[p], crsem.at[p], pair)
        copy.start()
        c_copies.append(copy)

    def v_copy(i, bit):
        return remote(
            piv.at[pl.ds(mine, vrows)], pivx.at[i], vsend.at[i + 1], vrecv.at[i + 1], (flip(scen, bit), col)
        )

    v0.wait()
    piv[pl.ds(mine, vrows)] = piv[pl.ds(mine, vrows)] + pivc[...]
    stages = scen_bits[1:]
    v_copies = [v_copy(i, b) for i, b in enumerate(stages)]
    if v_copies:
        v_copies[0].start()

    def x_copy(i, p):
        return remote(
            acc.at[p], xrecv.at[i, p], xsend.at[i, p], xrsem.at[i, p], (flip(scen, stages[i]), col)
        )

    for p in range(pieces):
        own = term(core * half + p * rows)
        c_copies[p].wait()
        acc[p] = own + crecv[p]
        if stages:
            x_copy(0, p).start()
    for i in range(len(stages)):
        v_copies[i].wait()
        piv[pl.ds(mine, vrows)] = piv[pl.ds(mine, vrows)] + pivx[i]
        if i + 1 < len(stages):
            v_copies[i + 1].start()
    vback = remote(
        piv.at[pl.ds(mine, vrows)], pivb, vsend.at[len(stages) + 1], vrecv.at[len(stages) + 1], pair
    )
    vback.start()
    for i in range(len(stages) - 1):
        for p in range(pieces):
            x_copy(i, p).wait()
            acc[p] = acc[p] + xrecv[i, p]
            x_copy(i + 1, p).start()
    vback.wait()
    piv[pl.ds(theirs, vrows)] = pivb[...]

    eye = lax.broadcasted_iota(jnp.int32, (HALF, HALF), 0) == lax.broadcasted_iota(
        jnp.int32, (HALF, HALF), 1
    )
    a00 = piv[0:HALF]
    a01 = piv[HALF : 2 * HALF]
    a11 = piv[2 * HALF : 3 * HALF]
    a00 = 0.5 * (a00 + a00.T) + jnp.where(eye, d_ref[0:1, :], 0.0)
    a11 = 0.5 * (a11 + a11.T) + jnp.where(eye, d_ref[1:2, :], 0.0)
    u00, inv0 = factor_block(a00)
    u01 = full(inv0, a01)
    l10 = u01.T
    u11, inv1 = factor_block(a11 - full(l10, u01))
    inv10 = -full(inv1, full(l10, inv0))
    zero = jnp.zeros((HALF, HALF), F32)
    inverse = jnp.concatenate(
        [jnp.concatenate([inv0, zero], axis=1), jnp.concatenate([inv10, inv1], axis=1)], axis=0
    )

    o_copies = []
    last = len(stages) - 1
    for p in range(pieces):
        value = acc[p]
        if stages:
            x_copy(last, p).wait()
            value = value + xrecv[last, p]
        start = pl.multiple_of(core * half + p * rows, rows)
        xout[pl.ds(start, rows)] = full(value, inverse, ((1,), (1,)))
        copy = remote(xout.at[pl.ds(start, rows)], xout.at[pl.ds(start, rows)], osend.at[p], orsem.at[p], pair)
        copy.start()
        o_copies.append(copy)
    for p in range(pieces):
        o_copies[p].wait_send()
        start = pl.multiple_of((1 - core) * half + p * rows, rows)
        remote(xout.at[pl.ds(start, rows)], xout.at[pl.ds(start, rows)], osend.at[p], orsem.at[p], pair).wait_recv()

    @pl.when(col == 0)
    def _():
        xout[0:HALF, 0:HALF] = u00.T
        xout[0:HALF, HALF:] = zero
        xout[HALF:PANEL, 0:HALF] = l10
        xout[HALF:PANEL, HALF:] = u11.T

    store = pltpu.make_async_copy(xout, out_ref, lsem.at[2])
    store.start()
    for copy in h_copies:
        copy.wait_send()
    for q in range(QUEUE):
        @pl.when(along)
        def _(q=q):
            p_copy(q, 0).wait_send()

        @pl.when(even)
        def _(q=q):
            p_copy(q, 1).wait_send()
    store.wait()


def shards(n_scen, n_col, coupling, inverse_slabs, barrier_diagonal):
    depth, n = coupling.shape[1:]
    pieces = 4
    half = n // 2
    rows = half // pieces
    stages = max((n_scen - 1).bit_length() - 1, 1)
    dma = pltpu.SemaphoreType.DMA
    return pl.pallas_call(
        functools.partial(kernel, n_scen, n_col, pieces),
        out_shape=jax.ShapeDtypeStruct((n, PANEL), F32),
        in_specs=[pl.BlockSpec(memory_space=pl.ANY)] * 2 + [pl.BlockSpec(memory_space=pltpu.VMEM)],
        out_specs=pl.BlockSpec(memory_space=pl.ANY),
        scratch_shapes=[
            pltpu.VMEM((depth, n), F32),
            pltpu.VMEM((depth, depth), F32),
            pltpu.VMEM((depth, PANEL), F32),
            pltpu.VMEM((n, depth), BF16),
            pltpu.VMEM((n, depth), BF16),
            pltpu.VMEM((pieces, rows, PANEL), F32),
            pltpu.VMEM((pieces, rows, PANEL), F32),
            pltpu.VMEM((pieces, rows, PANEL), F32),
            pltpu.VMEM((stages, pieces, rows, PANEL), F32),
            pltpu.VMEM((n, PANEL), F32),
            pltpu.VMEM((3 * HALF, HALF), F32),
            pltpu.VMEM((3 * HALF // 2, HALF), F32),
            pltpu.VMEM((3 * HALF // 2, HALF), F32),
            pltpu.VMEM((stages, 3 * HALF // 2, HALF), F32),
            dma((3,)),
            dma((n_col,)),
            dma((n_col,)),
            dma((QUEUE, 2)),
            dma((QUEUE,)),
            dma((pieces,)),
            dma((pieces,)),
            dma((stages, pieces)),
            dma((stages, pieces)),
            dma((pieces,)),
            dma((pieces,)),
            dma((stages + 2,)),
            dma((stages + 2,)),
        ],
        compiler_params=pltpu.CompilerParams(
            collective_id=0, has_side_effects=True, vmem_limit_bytes=40 * 1024 * 1024
        ),
    )(coupling, inverse_slabs, barrier_diagonal.reshape(-1, 128))


def solution(mesh):
    return jax.shard_map(
        functools.partial(shards, mesh.shape["scen"], mesh.shape["col"]),
        mesh=mesh,
        in_specs=(P("scen", None, "col"), P("scen", "col", None), P(None)),
        out_specs=P("col", None),
        check_vma=False,
    )
```

```python
import functools

import jax
import jax.numpy as jnp
from jax import lax
from jax.experimental import pallas as pl
from jax.experimental.pallas import tpu as pltpu
from jax.sharding import PartitionSpec as P

PANEL = 256
HALF = PANEL // 2
QUEUE = 8
MESH = pl.DeviceIdType.MESH
HI = lax.Precision.HIGHEST
F32 = jnp.float32
BF16 = jnp.bfloat16


def split(value):
    high = value.astype(BF16)
    return high, (value - high.astype(F32)).astype(BF16)


def dot(a, b):
    return jnp.dot(a, b, preferred_element_type=F32)


def full(a, b, dims=((1,), (0,))):
    return lax.dot_general(a, b, (dims, ((), ())), precision=HI, preferred_element_type=F32)


def factor_block(a, step=2):
    size = a.shape[0]
    row = lax.broadcasted_iota(jnp.int32, (size, size), 0)
    col = lax.broadcasted_iota(jnp.int32, (size, size), 1)
    left, right = a, jnp.where(row == col, 1.0, 0.0).astype(F32)
    for k in range(0, size, step):
        base = k // 8 * 8
        l_live, r_live = left[base:], right[base:]
        rows = lax.broadcasted_iota(jnp.int32, (size - base, 1), 0) + base
        cols = [
            jnp.broadcast_to(l_live[:, k + t : k + t + 1], (size - base, size)) for t in range(step)
        ]
        lrows = [l_live[k + t - base : k + t + 1 - base] for t in range(step)]
        rrows = [r_live[k + t - base : k + t + 1 - base] for t in range(step)]
        for t in range(step):
            at = k + t - base
            inv = 1.0 / cols[t][at : at + 1]
            fac = jnp.where(rows > k + t, cols[t] * inv, 0.0)
            for u in range(t + 1, step):
                au = k + u - base
                cols[u] = cols[u] - fac * cols[u][at : at + 1]
                lrows[u] = lrows[u] - fac[au : au + 1] * lrows[t]
                rrows[u] = rrows[u] - fac[au : au + 1] * rrows[t]
            l_live = l_live - fac * lrows[t]
            r_live = r_live - fac * rrows[t]
        if base:
            left = jnp.concatenate([left[:base], l_live], axis=0)
            right = jnp.concatenate([right[:base], r_live], axis=0)
        else:
            left, right = l_live, r_live
    diag = jnp.sum(jnp.where(row == col, left, 0.0), axis=1, keepdims=True)
    scale = 1.0 / jnp.sqrt(diag)
    return jnp.where(row <= col, left * scale, 0.0), right * scale


def kernel(
    n_scen, n_col, pieces, c_ref, h_ref, d_ref, out_ref,
    cbuf, dbuf, hbuf, pbuf, sbuf, chi, clo, sendbuf, acc, crecv, xrecv, xout,
    piv, pivc, pivb, pivx,
    lsem, ssend, srecv, psend, precv, csend, crsem, xsend, xrsem, osend, orsem, vsend, vrecv,
):
    scen, col = lax.axis_index("scen"), lax.axis_index("col")
    depth, n = cbuf.shape
    share = h_ref.shape[1]
    half = n // 2
    rows = half // pieces
    core = lax.rem(scen, 2)
    col_bits = [1 << i for i in reversed(range((n_col - 1).bit_length()))]
    scen_bits = [1 << i for i in range((n_scen - 1).bit_length())]

    def flip(index, bit):
        return jnp.where(lax.rem(index // bit, 2) == 0, index + bit, index - bit)

    def xor(index, mask):
        for b in col_bits:
            if mask & b:
                index = flip(index, b)
        return index

    def remote(src, dst, send, recv, who):
        return pltpu.make_async_remote_copy(
            src_ref=src, dst_ref=dst, send_sem=send, recv_sem=recv, device_id=who, device_id_type=MESH
        )

    load_c = pltpu.make_async_copy(c_ref.at[0], cbuf, lsem.at[0])
    load_d = pltpu.make_async_copy(d_ref.at[pl.ds(0, 8)], dbuf, lsem.at[3])
    load_h = pltpu.make_async_copy(h_ref.at[0], hbuf, lsem.at[1])

    def load_p(t):
        return pltpu.make_async_copy(c_ref.at[0, :, pl.ds(t * HALF, HALF)], pbuf.at[t], lsem.at[4 + t])

    @pl.when(col == 0)
    def _():
        load_p(0).start()
        load_p(1).start()

    load_h.start()
    load_c.start()
    load_d.start()

    barrier = pltpu.get_barrier_semaphore()
    peers = [(scen, flip(col, b)) for b in col_bits]
    peers += [(scen, lax.rem(col + 2, n_col)), (scen, lax.rem(col + n_col - 2, n_col))]
    peers += [(flip(scen, b), col) for b in scen_bits]
    for peer in peers:
        pl.semaphore_signal(barrier, inc=1, device_id=peer, device_id_type=MESH)
    pl.semaphore_wait(barrier, len(peers))

    s_copies = []

    def s_send(d):
        owner = xor(col, d)
        where = sbuf.at[pl.ds(pl.multiple_of(owner * share, share), share)]
        for b in col_bits:
            if d == 0 or b < (d & -d):
                copy = remote(where, where, ssend.at[len(s_copies)], srecv.at[d | b], (scen, flip(col, b)))
                copy.start()
                s_copies.append(copy)

    def s_wait(d):
        owner = xor(col, d)
        where = sbuf.at[pl.ds(pl.multiple_of(owner * share, share), share)]
        remote(where, where, ssend.at[0], srecv.at[d], (scen, flip(col, 1))).wait_recv()

    side, pair_at = lax.rem(col, 2), col // 2
    prow = depth // QUEUE
    ahead = pair_at + 1 < n_col // 2
    across = pair_at >= 1
    returns = col == 3

    def p_copy(t, q, slot, target):
        where = pbuf.at[t, pl.ds(q * prow, prow)]
        return remote(where, where, psend.at[slot, q], precv.at[t, q], (scen, target))

    def p_wait(t, q):
        p_copy(t, q, 0, flip(col, 1)).wait_recv()

    def p_ahead(q):
        return p_copy(side, q, 0, lax.rem(col + 2, n_col))

    def p_across(q):
        return p_copy(side, q, 1, flip(col, 1))

    def p_first(q):
        return p_copy(1, q, 1, flip(col, 1))

    def p_back(q):
        return p_copy(0, q, 2, lax.rem(col + n_col - 2, n_col))

    def transpose(j):
        high, low = split(cbuf[:, j * 128 : (j + 1) * 128].T)
        chi[j * 128 : (j + 1) * 128] = high
        clo[j * 128 : (j + 1) * 128] = low

    blocks = n // 128
    early = blocks // 2

    @pl.when(col == 0)
    def _():
        load_p(0).wait()
        load_p(1).wait()

    for q in range(QUEUE):
        @pl.when(col != 0)
        def _(q=q):
            p_wait(side, q)

        @pl.when(ahead)
        def _(q=q):
            p_ahead(q).start()

        @pl.when(across)
        def _(q=q):
            p_across(q).start()

        @pl.when(col == 0)
        def _(q=q):
            p_first(q).start()

        if q:
            @pl.when(returns)
            def _(q=q):
                p_wait(0, q - 1)
                p_back(q - 1).start()
        if q == 0:
            load_c.wait()
        for j in range(q * early // QUEUE, (q + 1) * early // QUEUE):
            transpose(j)

    @pl.when(returns)
    def _():
        p_wait(0, QUEUE - 1)
        p_back(QUEUE - 1).start()

    @pl.when(jnp.logical_and(col != 0, col != 3))
    def _():
        for q in range(QUEUE):
            p_wait(1 - side, q)

    load_h.wait()
    load_d.wait()
    panel = jnp.concatenate([pbuf[0], pbuf[1]], axis=1)
    sbuf[pl.ds(pl.multiple_of(col * share, share), share)] = full(hbuf[...], panel)
    s_send(0)
    panel_t = panel.T
    order = sorted(range(1, n_col), key=lambda d: (bin(d).count("1"), -d))
    for i, d in enumerate(order):
        s_wait(d)
        s_send(d)
        late = blocks - early
        for j in range(early + i * late // len(order), early + (i + 1) * late // len(order)):
            transpose(j)

    solved = sbuf[...]
    s_hi, s_lo = split(solved)
    top = full(panel_t[:HALF], solved)
    piv[0:HALF] = top[:, :HALF]
    piv[HALF : 2 * HALF] = top[:, HALF:]
    piv[2 * HALF : 3 * HALF] = full(panel_t[HALF:], solved[:, HALF:])
    vrows = 3 * HALF // 2
    mine = pl.multiple_of(core * vrows, vrows)
    theirs = pl.multiple_of((1 - core) * vrows, vrows)
    pair = (flip(scen, 1), col)
    v0 = remote(piv.at[pl.ds(theirs, vrows)], pivc, vsend.at[0], vrecv.at[0], pair)
    v0.start()

    def term(start):
        start = pl.multiple_of(start, rows)
        high, low = chi[pl.ds(start, rows)], clo[pl.ds(start, rows)]
        return dot(high, s_hi) + (dot(high, s_lo) + dot(low, s_hi))

    c_copies = []
    for p in range(pieces):
        sendbuf[p] = term((1 - core) * half + p * rows)
        copy = remote(sendbuf.at[p], crecv.at[p], csend.at[p], crsem.at[p], pair)
        copy.start()
        c_copies.append(copy)

    def v_copy(i, bit):
        return remote(
            piv.at[pl.ds(mine, vrows)], pivx.at[i], vsend.at[i + 1], vrecv.at[i + 1], (flip(scen, bit), col)
        )

    v0.wait()
    piv[pl.ds(mine, vrows)] = piv[pl.ds(mine, vrows)] + pivc[...]
    stages = scen_bits[1:]
    v_copies = [v_copy(i, b) for i, b in enumerate(stages)]
    if v_copies:
        v_copies[0].start()

    def x_copy(i, p):
        return remote(
            acc.at[p], xrecv.at[i, p], xsend.at[i, p], xrsem.at[i, p], (flip(scen, stages[i]), col)
        )

    for p in range(pieces):
        own = term(core * half + p * rows)
        c_copies[p].wait()
        acc[p] = own + crecv[p]
        if stages:
            x_copy(0, p).start()
    for i in range(len(stages)):
        v_copies[i].wait()
        piv[pl.ds(mine, vrows)] = piv[pl.ds(mine, vrows)] + pivx[i]
        if i + 1 < len(stages):
            v_copies[i + 1].start()
    vback = remote(
        piv.at[pl.ds(mine, vrows)], pivb, vsend.at[len(stages) + 1], vrecv.at[len(stages) + 1], pair
    )
    vback.start()
    for i in range(len(stages) - 1):
        for p in range(pieces):
            x_copy(i, p).wait()
            acc[p] = acc[p] + xrecv[i, p]
            x_copy(i + 1, p).start()
    vback.wait()
    piv[pl.ds(theirs, vrows)] = pivb[...]

    eye = lax.broadcasted_iota(jnp.int32, (HALF, HALF), 0) == lax.broadcasted_iota(
        jnp.int32, (HALF, HALF), 1
    )
    a00 = piv[0:HALF]
    a01 = piv[HALF : 2 * HALF]
    a11 = piv[2 * HALF : 3 * HALF]
    a00 = 0.5 * (a00 + a00.T) + jnp.where(eye, dbuf[0:1, :], 0.0)
    a11 = 0.5 * (a11 + a11.T) + jnp.where(eye, dbuf[1:2, :], 0.0)
    u00, inv0 = factor_block(a00)
    u01 = full(inv0, a01)
    l10 = u01.T
    u11, inv1 = factor_block(a11 - full(l10, u01))
    inv10 = -full(inv1, full(l10, inv0))
    zero = jnp.zeros((HALF, HALF), F32)
    inverse = jnp.concatenate(
        [jnp.concatenate([inv0, zero], axis=1), jnp.concatenate([inv10, inv1], axis=1)], axis=0
    )

    o_copies = []
    last = len(stages) - 1
    for p in range(pieces):
        value = acc[p]
        if stages:
            x_copy(last, p).wait()
            value = value + xrecv[last, p]
        start = pl.multiple_of(core * half + p * rows, rows)
        xout[pl.ds(start, rows)] = full(value, inverse, ((1,), (1,)))
        copy = remote(xout.at[pl.ds(start, rows)], xout.at[pl.ds(start, rows)], osend.at[p], orsem.at[p], pair)
        copy.start()
        o_copies.append(copy)
    for p in range(pieces):
        o_copies[p].wait_send()
        start = pl.multiple_of((1 - core) * half + p * rows, rows)
        remote(xout.at[pl.ds(start, rows)], xout.at[pl.ds(start, rows)], osend.at[p], orsem.at[p], pair).wait_recv()

    @pl.when(col == 0)
    def _():
        xout[0:HALF, 0:HALF] = u00.T
        xout[0:HALF, HALF:] = zero
        xout[HALF:PANEL, 0:HALF] = l10
        xout[HALF:PANEL, HALF:] = u11.T

    store = pltpu.make_async_copy(xout, out_ref, lsem.at[2])
    store.start()
    for copy in s_copies:
        copy.wait_send()
    for q in range(QUEUE):
        @pl.when(ahead)
        def _(q=q):
            p_ahead(q).wait_send()

        @pl.when(across)
        def _(q=q):
            p_across(q).wait_send()

        @pl.when(col == 0)
        def _(q=q):
            p_first(q).wait_send()

        @pl.when(returns)
        def _(q=q):
            p_back(q).wait_send()
    store.wait()


def shards(n_scen, n_col, coupling, inverse_slabs, barrier_diagonal):
    depth, n = coupling.shape[1:]
    pieces = 4
    half = n // 2
    rows = half // pieces
    stages = max((n_scen - 1).bit_length() - 1, 1)
    dma = pltpu.SemaphoreType.DMA
    return pl.pallas_call(
        functools.partial(kernel, n_scen, n_col, pieces),
        out_shape=jax.ShapeDtypeStruct((n, PANEL), F32),
        in_specs=[pl.BlockSpec(memory_space=pltpu.HBM)] * 3,
        out_specs=pl.BlockSpec(memory_space=pl.ANY),
        scratch_shapes=[
            pltpu.VMEM((depth, n), F32),
            pltpu.VMEM((8, 128), F32),
            pltpu.VMEM((inverse_slabs.shape[1], depth), F32),
            pltpu.VMEM((2, depth, HALF), F32),
            pltpu.VMEM((depth, PANEL), F32),
            pltpu.VMEM((n, depth), BF16),
            pltpu.VMEM((n, depth), BF16),
            pltpu.VMEM((pieces, rows, PANEL), F32),
            pltpu.VMEM((pieces, rows, PANEL), F32),
            pltpu.VMEM((pieces, rows, PANEL), F32),
            pltpu.VMEM((stages, pieces, rows, PANEL), F32),
            pltpu.VMEM((n, PANEL), F32),
            pltpu.VMEM((3 * HALF, HALF), F32),
            pltpu.VMEM((3 * HALF // 2, HALF), F32),
            pltpu.VMEM((3 * HALF // 2, HALF), F32),
            pltpu.VMEM((stages, 3 * HALF // 2, HALF), F32),
            dma((6,)),
            dma((n_col,)),
            dma((n_col,)),
            dma((3, QUEUE)),
            dma((2, QUEUE)),
            dma((pieces,)),
            dma((pieces,)),
            dma((stages, pieces)),
            dma((stages, pieces)),
            dma((pieces,)),
            dma((pieces,)),
            dma((stages + 2,)),
            dma((stages + 2,)),
        ],
        compiler_params=pltpu.CompilerParams(
            collective_id=0, has_side_effects=True, vmem_limit_bytes=40 * 1024 * 1024
        ),
    )(coupling, inverse_slabs, barrier_diagonal.reshape(-1, 128))


def solution(mesh):
    return jax.shard_map(
        functools.partial(shards, mesh.shape["scen"], mesh.shape["col"]),
        mesh=mesh,
        in_specs=(P("scen", None, "col"), P("scen", "col", None), P(None)),
        out_specs=P("col", None),
        check_vma=False,
    )
```
